1024 devices in a mesh: fsdp: 32 (over y, x), rep: 32 (over z, core).
Axes of the slice: x: 4, y: 8, z: 16, core: 2. Of those that a mesh axis runs over, the one named last changes fastest.
Arguments:
- gradient: bfloat16 [8, 128, 512, 128], P(None, 'rep', 'fsdp'), may hold values from -25 to 25
- momentum: bfloat16 [32, 64, 512, 128], P('rep', 'fsdp'), may hold values from -6 to 6
- owners: int32 [128, 8, 1], P('rep'), may hold values from 0 to 31; in each aligned block of 32 rows (0 to 31, 32 to 63, ..., all dimensions but the last counted through in order) at most 2 rows name the same one
Outputs:
- update: bfloat16 [8, 128, 512, 128], P(None, None, 'fsdp')
- momentum_new: bfloat16 [32, 64, 512, 128], P('rep', 'fsdp')
The draws below stay inside these ranges and needn't reach their ends.
Inputs may be any that keep to these rules, and one draw needn't show every extreme that they name: `owners`: among the head blocks of one rep index (all layers), no owner is named by more than 2 blocks, and in some rep index one owner is named by exactly 2 blocks.
All inputs are finite; a program needn't handle non-finite values.
Results may differ from the reference program's by a relative error of at most 0.001.
Values may be sent and summed in bfloat16 or wider, within the bound.
A program may use at most 32 MiB of HBM per device.

```python
import math
import jax
import jax.numpy as jnp
import numpy as np
from jax import lax

LAYERS = 8
RANK = 512
BLOCK = 128
BLOCKS = 128
ITERS = 5
CAP = 2
N_FSDP = 32
N_REP = 32


def draw_gradient(key, part):
    key = jax.random.fold_in(key, 7)
    key_base, key_scale = jax.random.split(key, 2)
    shape = (LAYERS, BLOCKS, RANK, BLOCK)
    base = jnp.clip(jax.random.normal(key_base, shape, jnp.float32), -6.0, 6.0)
    spread = jnp.exp(jax.random.uniform(key_scale, (LAYERS, 1, RANK, 1), jnp.float32) * math.log(10.0))
    values = base * spread
    return (values / 3.0).astype(jnp.bfloat16)


def block_scale(own_key, extent, pieces, least, high):
    gain = 1.0
    for dim, parts in pieces:
        draws = jax.random.uniform(jax.random.fold_in(jax.random.fold_in(own_key, 6), dim), (parts,), jnp.float32, least / len(pieces), high / len(pieces))
        gain = gain * jnp.repeat(jnp.exp(draws), extent[dim] // parts).reshape((-1,) + (1,) * (len(extent) - 1 - dim))
    return gain


def deal_out(key, own, number, rows, amount, top, reach, slope):
    ranking = jax.random.permutation(key, amount)
    crowded, ordinary = shares(amount, rows * top, reach, slope, True), shares(amount, rows * top, reach, slope, False)
    places = jnp.arange(amount)

    def named(lengths, turn):
        used = int((lengths > 0).sum())
        fixed = max(1, used // 4)
        passed = fixed + (places - fixed + turn * (used - fixed)) % max(1, amount - fixed)
        return jnp.zeros((amount,), jnp.int32).at[ranking[jnp.where(places < fixed, places, passed)]].set(jnp.asarray(lengths, jnp.int32))

    lengths = jnp.where(number % 4 == 0, named(crowded, number // 4), named(ordinary, number - number // 4 - 1))
    mixed = jax.random.permutation(jax.random.fold_in(own, 3), amount)
    giver, sink = mixed[0:amount // 2 * 2:2], mixed[1:amount // 2 * 2:2]
    slack = jnp.minimum(lengths[giver] - 1, reach - lengths[sink]) // 2
    slack = jnp.where((giver == ranking[0]) | (sink == ranking[0]) | (lengths[sink] == 0), 0, jnp.maximum(slack, 0))
    passed = jax.random.randint(jax.random.fold_in(own, 4), (amount // 2,), 0, 1 << 20) % (slack + 1)
    lengths = lengths.at[giver].add(-passed).at[sink].add(passed)
    items = jnp.searchsorted(jnp.cumsum(lengths), jnp.arange(rows * top), side="right").astype(jnp.int32)
    grid = items.reshape(top, rows).T
    grid = grid[jax.random.permutation(jax.random.fold_in(own, 1), rows)]
    turn = jax.random.randint(jax.random.fold_in(own, 2), (rows, 1), 0, top)
    return jnp.take_along_axis(grid, (jnp.arange(top)[None, :] + turn) % top, axis=1)


def shares(number_of, total, reach, lean, full):
    loads = [(1 << 20) // math.isqrt(rank ** lean) + 1 for rank in range(1, number_of + 1)]
    largest = reach if full else min(reach, max(-(-total // number_of), total * loads[0] // sum(loads)))
    least = 1 if total - largest >= number_of - 1 else 0
    holding, rest = [largest] + [least] * (number_of - 1), total - largest - least * (number_of - 1)
    while rest > 0:
        candidates = [i for i in range(1, number_of) if holding[i] < largest] or [i for i in range(1, number_of) if holding[i] < reach]
        mass, left = sum([loads[i] for i in candidates]), rest
        for i in candidates:
            extra = min(reach - holding[i], max(1, left * loads[i] // mass), rest)
            holding[i] = holding[i] + extra
            rest = rest - extra
    return np.array(holding)


def normal_values(key, shape, width, reach, cuts=(), kind=jnp.bfloat16):
    array = width * jax.random.normal(key, shape, jnp.float32)
    if cuts:
        array = array * block_scale(key, shape, cuts, -0.22, 0.18)
    return jnp.clip(array, -reach, reach).astype(kind)


def setup_inputs(seed: int = 0) -> dict:
    keys = jax.random.split(jax.random.key(seed), 4)
    gradient = draw_gradient(jax.random.fold_in(keys[3], 71), 0)
    momentum = normal_values(keys[1], (N_REP, N_FSDP * CAP, RANK, BLOCK), 1.0, 6.0, ((0, 32), (1, 32)))
    owners_keys = jax.random.split(jax.random.fold_in(keys[2], 1), BLOCKS * LAYERS // (LAYERS * (BLOCKS // N_REP)))
    owners_turns = jax.random.permutation(jax.random.fold_in(keys[2], 3), BLOCKS * LAYERS // (LAYERS * (BLOCKS // N_REP)))
    owners = jax.vmap(lambda own, number: deal_out(jax.random.fold_in(keys[2], 2), own, number, LAYERS * (BLOCKS // N_REP), N_FSDP, 1, CAP, 2))(owners_keys, owners_turns).reshape((BLOCKS, LAYERS, 1))
    return dict(gradient=gradient, momentum=momentum, owners=owners)


beta_decay = 0.95
coef_a = 3.4445
coef_b = -4.775
coef_c = 2.0315
epsilon = 1e-07

def orthogonalize(blend):
    frob_norm = jnp.sqrt(lax.optimization_barrier(jnp.sum(blend * blend, axis=(1, 2), keepdims=True)))
    current = blend / (frob_norm + epsilon)
    for step in range(ITERS):
        gram_mat = jnp.einsum('kcr,kcs->krs', current, current, precision=lax.Precision.HIGHEST)
        polynom = coef_b * gram_mat + coef_c * jnp.einsum('krs,kst->krt', gram_mat, gram_mat, precision=lax.Precision.HIGHEST)
        current = coef_a * current + jnp.einsum('kcr,krs->kcs', current, polynom, precision=lax.Precision.HIGHEST)
    return current

def reference(gradient, momentum, owners):
    blk_local = BLOCKS // N_REP
    flat_rows = LAYERS * blk_local
    muon_scale = 0.2 * math.sqrt(max(RANK, BLOCK))

    def per_group(group_index):
        grad_group = lax.dynamic_slice_in_dim(gradient, group_index * blk_local, blk_local, 1)
        owner_group = lax.dynamic_slice_in_dim(owners, group_index * blk_local, blk_local, 0)
        owner_flat = jnp.transpose(owner_group[:, :, 0]).reshape(flat_rows)
        onehot_owner = (owner_flat[:, None] == jnp.arange(N_FSDP, dtype=jnp.int32)[None, :]).astype(jnp.int32)
        rank_within = jnp.cumsum(onehot_owner, axis=0) - 1
        slot_of = lax.optimization_barrier(jnp.sum(rank_within * onehot_owner, axis=1)).astype(jnp.int32)
        position = (owner_flat * CAP + slot_of).astype(jnp.int32)
        prior = lax.dynamic_index_in_dim(momentum, group_index, 0, keepdims=False).astype(jnp.float32)
        fresh = jnp.zeros_like(prior).at[position].set(grad_group.reshape(flat_rows, RANK, BLOCK).astype(jnp.float32))
        carried = beta_decay * prior + fresh
        blend = (fresh + beta_decay * carried)[position]
        update_rows = (muon_scale * orthogonalize(blend)).astype(jnp.bfloat16)
        return (carried.astype(jnp.bfloat16), update_rows.reshape(LAYERS, blk_local, RANK, BLOCK))
    momentum_new, update_groups = lax.map(per_group, jnp.arange(N_REP, dtype=jnp.int32))
    update = jnp.transpose(update_groups, (1, 0, 2, 3, 4)).reshape(LAYERS, BLOCKS, RANK, BLOCK)
    return (update, momentum_new)
```

```python
import math

import jax
import jax.numpy as jnp
from jax import lax
from jax.experimental import pallas as pl
from jax.experimental.pallas import tpu as pltpu
from jax.sharding import PartitionSpec as P

RANK = 512
BLOCK = 128
ITERS = 5
CHIPS = 16
PIECES = 4
STEPS = 7


beta_decay = 0.95
coef_a = 3.4445
coef_b = -4.775
coef_c = 2.0315
epsilon = 1e-07


def gather_kernel(mine_ref, out_ref, go_sem, come_sem, give_sem, take_sem, own_sem):
    rep = lax.axis_index("rep")
    core = lax.rem(rep, 2)
    chip = lax.div(rep, 2)
    up = lax.rem(chip + 1, CHIPS) * 2 + core
    down = lax.rem(chip + CHIPS - 1, CHIPS) * 2 + core
    twin = chip * 2 + 1 - core
    targets = (up, down)
    layers, held = mine_ref.shape[:2]
    depth = layers // PIECES

    barrier = pltpu.get_barrier_semaphore()
    for other in (up, down, twin):
        pl.semaphore_signal(barrier, inc=1, device_id={"rep": other}, device_id_type=pl.DeviceIdType.MESH)
    pl.semaphore_wait(barrier, 3)

    def place(where, piece):
        return out_ref.at[pl.ds(piece * depth, depth), pl.ds(where * held, held)]

    def hop(way, step, piece, own):
        if way == 0:
            at = lax.rem(chip + CHIPS - step, CHIPS)
        else:
            at = lax.rem(chip + step, CHIPS)
        dst = place(at * 2 + core, piece)
        src = mine_ref.at[pl.ds(piece * depth, depth)] if own else dst
        return pltpu.make_async_remote_copy(
            src_ref=src, dst_ref=dst,
            send_sem=go_sem.at[way, step, piece], recv_sem=come_sem.at[way, step, piece],
            device_id={"rep": targets[way]}, device_id_type=pl.DeviceIdType.MESH)

    def share(slot, at, piece, own):
        dst = place(at * 2 + core, piece)
        src = mine_ref.at[pl.ds(piece * depth, depth)] if own else dst
        return pltpu.make_async_remote_copy(
            src_ref=src, dst_ref=dst,
            send_sem=give_sem.at[slot, piece], recv_sem=take_sem.at[slot, piece],
            device_id={"rep": twin}, device_id_type=pl.DeviceIdType.MESH)

    for piece in range(PIECES):
        for way in range(2):
            hop(way, 0, piece, True).start()
    for piece in range(PIECES):
        share(0, chip, piece, True).start()
    own = pltpu.make_async_copy(mine_ref, out_ref.at[:, pl.ds(rep * held, held)], own_sem)
    own.start()

    def arrived(way, step, piece):
        hop(way, step, piece, False).wait_recv()
        if way == 0:
            at = lax.rem(chip + CHIPS - 1 - step, CHIPS)
        else:
            at = lax.rem(chip + 1 + step, CHIPS)
        return at

    @pl.loop(0, STEPS - 1)
    def _(step):
        for piece in range(PIECES):
            for way in range(2):
                at = arrived(way, step, piece)
                hop(way, step + 1, piece, False).start()
                share(1 + 2 * step + way, at, piece, False).start()

    last = STEPS - 1
    for piece in range(PIECES):
        for way in range(2):
            at = arrived(way, last, piece)
            if piece % 2 == way:
                hop(way, last + 1, piece, False).start()
            share(1 + 2 * last + way, at, piece, False).start()
    for piece in range(PIECES):
        at = arrived(piece % 2, STEPS, piece)
        share(1 + 2 * STEPS, at, piece, False).start()

    own.wait()

    @pl.loop(0, STEPS)
    def _(step):
        for piece in range(PIECES):
            for way in range(2):
                hop(way, step, piece, False).wait_send()

    for piece in range(PIECES):
        hop(piece % 2, STEPS, piece, False).wait_send()

    @pl.loop(0, 2 * STEPS + 2)
    def _(slot):
        for piece in range(PIECES):
            both = share(slot, chip, piece, False)
            both.wait_send()
            both.wait_recv()


def gather(mine):
    layers, held, depth, width = mine.shape
    return pl.pallas_call(
        gather_kernel,
        out_shape=jax.ShapeDtypeStruct((layers, held * 2 * CHIPS, depth, width), mine.dtype),
        in_specs=[pl.BlockSpec(memory_space=pltpu.VMEM)],
        out_specs=pl.BlockSpec(memory_space=pltpu.VMEM),
        scratch_shapes=[
            pltpu.SemaphoreType.DMA((2, STEPS + 1, PIECES)),
            pltpu.SemaphoreType.DMA((2, STEPS + 1, PIECES)),
            pltpu.SemaphoreType.DMA((2 * STEPS + 2, PIECES)),
            pltpu.SemaphoreType.DMA((2 * STEPS + 2, PIECES)),
            pltpu.SemaphoreType.DMA,
        ],
        compiler_params=pltpu.CompilerParams(
            collective_id=1, has_side_effects=True, vmem_limit_bytes=32 * 2**20),
        cost_estimate=pl.CostEstimate(flops=0, bytes_accessed=2**22, transcendentals=0),
    )(mine)


def orthogonalize(blend):
    frob_norm = jnp.sqrt(jnp.sum(blend * blend, axis=(1, 2), keepdims=True))
    current = blend / (frob_norm + epsilon)
    for step in range(ITERS):
        gram_mat = jnp.einsum("kcr,kcs->krs", current, current, precision=lax.Precision.HIGHEST)
        polynom = coef_b * gram_mat + coef_c * jnp.einsum(
            "krs,kst->krt", gram_mat, gram_mat, precision=lax.Precision.HIGHEST
        )
        current = coef_a * current + jnp.einsum(
            "kcr,krs->kcs", current, polynom, precision=lax.Precision.HIGHEST
        )
    return current


def local(gradient, momentum, owners):
    layers, blk_local, col_count, rows_head = gradient.shape
    slot_count = momentum.shape[1]
    fsdp_count = lax.axis_size("fsdp")
    flat_rows = layers * blk_local
    muon_scale = 0.2 * math.sqrt(max(RANK, BLOCK))
    owner_flat = jnp.transpose(owners[:, :, 0]).reshape(flat_rows)
    onehot_owner = (owner_flat[:, None] == jnp.arange(fsdp_count, dtype=jnp.int32)[None, :]).astype(
        jnp.int32
    )
    rank_within = jnp.cumsum(onehot_owner, axis=0) - 1
    slot_of = jnp.sum(rank_within * onehot_owner, axis=1)
    target = slot_of * fsdp_count + owner_flat
    placing = (
        target[None, :] == jnp.arange(slot_count * fsdp_count, dtype=jnp.int32)[:, None]
    ).astype(jnp.bfloat16)
    pieces = gradient.reshape(flat_rows, col_count * rows_head)
    packed = jnp.dot(placing, pieces, preferred_element_type=jnp.float32).astype(jnp.bfloat16)
    packed = packed.reshape(slot_count, fsdp_count * col_count, rows_head)
    blocks = lax.all_to_all(packed, "fsdp", split_axis=1, concat_axis=1, tiled=True)
    prior = momentum[0].astype(jnp.float32)
    fresh = blocks.astype(jnp.float32)
    carried = beta_decay * prior + fresh
    momentum_new = carried.astype(jnp.bfloat16)[None]
    blend = fresh + beta_decay * carried
    owned_update = (muon_scale * orthogonalize(blend)).astype(jnp.bfloat16)
    back_target = owner_flat * slot_count + slot_of
    unplace = (
        back_target[None, :] == jnp.arange(fsdp_count * slot_count, dtype=jnp.int32)[:, None]
    ).astype(jnp.bfloat16)
    returned = lax.all_to_all(owned_update, "fsdp", split_axis=1, concat_axis=0, tiled=True)
    unpacked = jnp.einsum(
        "qr,qcb->rcb", unplace, returned, preferred_element_type=jnp.float32
    ).astype(jnp.bfloat16)
    update = gather(unpacked.reshape(layers, blk_local, col_count, returned.shape[2]))
    return (update, momentum_new)


def solution(mesh):
    placed = (P(None, "rep", "fsdp", None), P("rep", "fsdp", None, None), P("rep", None, None))
    return jax.shard_map(
        local,
        mesh=mesh,
        in_specs=placed,
        out_specs=(P(None, None, "fsdp", None), P("rep", "fsdp", None, None)),
        check_vma=False,
    )
```

```python
import functools
import math

import jax
import jax.numpy as jnp
from jax import lax
from jax.experimental import pallas as pl
from jax.experimental.pallas import tpu as pltpu
from jax.sharding import PartitionSpec as P

RANK = 512
BLOCK = 128
ROWS_Y = 8
ROWS_X = 4
CHIPS = 16
PIECES = 8
STEPS = 7
SEGMENTS = (3, 2)

beta_decay = 0.95
coef_a = 3.4445
coef_b = -4.775
coef_c = 2.0315
epsilon = 1e-07
muon_scale = 0.2 * math.sqrt(max(RANK, BLOCK))

F32 = jnp.float32
BF16 = jnp.bfloat16
MESH = pl.DeviceIdType.MESH
OFFSETS = sorted(
    [(y, x) for y in range(ROWS_Y) for x in range(ROWS_X) if (y, x) != (0, 0)],
    key=lambda o: -(min(o[0], ROWS_Y - o[0]) + min(o[1], ROWS_X - o[1])),
)


def split(value):
    high = value.astype(BF16)
    rest = value - high.astype(F32)
    mid = rest.astype(BF16)
    low = (rest - mid.astype(F32)).astype(BF16)
    return high, mid, low


def product(left, right):
    lh, lm, ll = left
    rh, rm, rl = right
    wide = jnp.concatenate([rh, rm], axis=1)
    main = jnp.dot(
        jnp.concatenate([lh, lm], axis=1), jnp.concatenate([wide, wide], axis=0), preferred_element_type=F32
    )
    rest = jnp.dot(
        jnp.concatenate([lh, ll], axis=1), jnp.concatenate([rl, rh], axis=0), preferred_element_type=F32
    )
    return main[:, :BLOCK] + (main[:, BLOCK:] + rest)


def gram(parts):
    high, mid, low = parts
    both = jnp.concatenate([high, mid], axis=1)
    dims = (((0,), (0,)), ((), ()))
    main = lax.dot_general(both, both, dims, preferred_element_type=F32)
    rest = lax.dot_general(high, low, dims, preferred_element_type=F32)
    cross = main[:BLOCK, BLOCK:] + main[BLOCK:, :BLOCK]
    return main[:BLOCK, :BLOCK] + (cross + (main[BLOCK:, BLOCK:] + (rest + rest.T)))


def orthogonalize(blends):
    row = lax.broadcasted_iota(jnp.int32, (BLOCK, BLOCK), 0)
    col = lax.broadcasted_iota(jnp.int32, (BLOCK, BLOCK), 1)
    eye = coef_a * (row == col).astype(F32)
    currents = []
    for blend in blends:
        total = jnp.sum(blend * blend, axis=(0, 1), keepdims=True)
        currents.append(blend / (jnp.sqrt(total) + epsilon))
    for count in SEGMENTS:
        parts = [split(y) for y in currents]
        grams = [gram(p) for p in parts]
        factors = None
        for step in range(count):
            pieces = [split(g) for g in grams]
            squares = [product(p, p) for p in pieces]
            polys = [split(eye + coef_b * g + coef_c * s) for g, s in zip(grams, squares)]
            if step < count - 1:
                halves = [product(p, r) for p, r in zip(pieces, polys)]
                grams = [product(split(h), r) for h, r in zip(halves, polys)]
            if factors is None:
                factors = polys
            else:
                factors = [split(product(f, r)) for f, r in zip(factors, polys)]
        currents = [product(p, f) for p, f in zip(parts, factors)]
    return currents


def kernel(
    owner_ref, gradient_ref, momentum_ref, update_ref, new_ref,
    packed, blocks, owned, returned, spread,
    out_sem, in_sem, back_sem, home_sem, self_sem,
    go_sem, come_sem, give_sem, take_sem, first_sem,
):
    rep = lax.axis_index("rep")
    me = lax.axis_index("fsdp")
    core = lax.rem(rep, 2)
    chip = lax.div(rep, 2)
    way = 1 - 2 * core
    ahead = lax.rem(chip + way + CHIPS, CHIPS) * 2 + core
    behind = lax.rem(chip - way + CHIPS, CHIPS) * 2 + core
    twin = chip * 2 + 1 - core
    mine_y = lax.div(me, ROWS_X)
    mine_x = lax.rem(me, ROWS_X)
    fsdp_count, slot_count, depth, width = packed.shape
    layers, _, _, _ = gradient_ref.shape
    held = gradient_ref.shape[1]
    flat_rows = layers * held
    block_rows = flat_rows * depth
    slot_rows = fsdp_count * slot_count * depth

    def peer(offset):
        return lax.rem(mine_y + offset[0], ROWS_Y) * ROWS_X + lax.rem(mine_x + offset[1], ROWS_X)

    barrier = pltpu.get_barrier_semaphore()
    for offset in OFFSETS:
        pl.semaphore_signal(barrier, inc=1, device_id={"fsdp": peer(offset)}, device_id_type=MESH)
    for other in (ahead, behind, twin):
        pl.semaphore_signal(barrier, inc=1, device_id={"rep": other}, device_id_type=MESH)

    names = [owner_ref[j % held, j // held] for j in range(flat_rows)]

    def targets(shape, dim):
        at = lax.broadcasted_iota(jnp.int32, shape, dim)
        number = at // depth
        owner = jnp.zeros(shape, jnp.int32)
        for j in range(flat_rows):
            owner = jnp.where(number == j, names[j], owner)
        slot = jnp.zeros(shape, jnp.int32)
        for j in range(flat_rows):
            slot += jnp.where((number > j) & (owner == names[j]), 1, 0)
        return (owner * slot_count + slot) * depth + lax.rem(at, depth)

    across = targets((1, block_rows), 1)
    place = (lax.broadcasted_iota(jnp.int32, (slot_rows, block_rows), 0) == across).astype(F32).astype(BF16)
    packed[...] = jnp.dot(
        place, gradient_ref[...].reshape(block_rows, width), preferred_element_type=F32
    ).astype(BF16).reshape(packed.shape)

    pl.semaphore_wait(barrier, len(OFFSETS) + 3)

    def swap(source, landing, sent, got, offset):
        other = peer(offset)
        return pltpu.make_async_remote_copy(
            src_ref=source.at[other], dst_ref=landing.at[me], send_sem=sent, recv_sem=got,
            device_id={"fsdp": other}, device_id_type=MESH)

    def exchange(source, landing, sent, got):
        for offset in OFFSETS:
            swap(source, landing, sent, got, offset).start()
        stays = pltpu.make_async_copy(source.at[me], landing.at[me], self_sem)
        stays.start()
        return stays

    def finish(landing, sent, got, stays):
        stays.wait()
        other = peer(OFFSETS[0])
        whole = landing.at[pl.ds(0, len(OFFSETS))]
        every = pltpu.make_async_remote_copy(
            src_ref=whole, dst_ref=whole, send_sem=sent, recv_sem=got,
            device_id={"fsdp": other}, device_id_type=MESH)
        every.wait_recv()
        every.wait_send()

    stays = exchange(packed, blocks, out_sem, in_sem)
    down = targets((block_rows, 1), 0)
    spread[...] = (lax.broadcasted_iota(jnp.int32, (block_rows, slot_rows), 1) == down).astype(F32).astype(BF16)
    finish(blocks, out_sem, in_sem, stays)

    blends = []
    for slot in range(slot_count):
        fresh = blocks[:, slot].reshape(RANK, width).astype(F32)
        carried = beta_decay * momentum_ref[0, slot].astype(F32) + fresh
        new_ref[0, slot] = carried.astype(BF16)
        blends.append(fresh + beta_decay * carried)
    for slot, current in enumerate(orthogonalize(blends)):
        owned[:, slot] = (muon_scale * current).astype(BF16).reshape(fsdp_count, depth, width)

    stays = exchange(owned, returned, back_sem, home_sem)
    finish(returned, back_sem, home_sem, stays)

    update_ref[:, pl.ds(rep * held, held)] = jnp.dot(
        spread[...], returned[...].reshape(slot_rows, width), preferred_element_type=F32
    ).astype(BF16).reshape(layers, held, depth, width)

    part = layers // PIECES

    def chunk(back, other):
        from_chip = lax.rem(chip - back * way + 2 * CHIPS, CHIPS)
        return from_chip * 2 + (core if other == 0 else 1 - core)

    def where(number, piece):
        return update_ref.at[pl.ds(piece * part, part), pl.ds(number * held, held)]

    def hop(step, other, piece):
        at = where(chunk(step, other), piece)
        return pltpu.make_async_remote_copy(
            src_ref=at, dst_ref=at, send_sem=go_sem, recv_sem=come_sem.at[step, other, piece],
            device_id={"rep": ahead}, device_id_type=MESH)

    def share(number, piece, sem):
        at = where(number, piece)
        return pltpu.make_async_remote_copy(
            src_ref=at, dst_ref=at, send_sem=give_sem, recv_sem=sem,
            device_id={"rep": twin}, device_id_type=MESH)

    for piece in range(PIECES):
        share(rep, piece, first_sem.at[piece]).start()
        hop(0, 0, piece).start()
    for piece in range(PIECES):
        share(rep, piece, first_sem.at[piece]).wait_recv()
        hop(0, 1, piece).start()

    @pl.loop(0, STEPS - 1)
    def _(step):
        for other in range(2):
            for piece in range(PIECES):
                hop(step, other, piece).wait_recv()
                hop(step + 1, other, piece).start()
                share(chunk(step + 1, other), piece, take_sem).start()

    last = STEPS - 1
    for other in range(2):
        for piece in range(PIECES):
            hop(last, other, piece).wait_recv()
            if other == 0:
                hop(STEPS, other, piece).start()
            share(chunk(STEPS, other), piece, take_sem).start()
    for piece in range(PIECES):
        hop(STEPS, 0, piece).wait_recv()
        share(chunk(STEPS + 1, 0), piece, take_sem).start()

    def chunks(number, sent, got):
        some = update_ref.at[:, pl.ds(0, number * held)]
        return pltpu.make_async_remote_copy(
            src_ref=some, dst_ref=some, send_sem=sent, recv_sem=got,
            device_id={"rep": twin}, device_id_type=MESH)

    chunks(2 * STEPS + 1, give_sem, take_sem).wait_recv()
    chunks(2 * STEPS + 1, go_sem, take_sem).wait_send()
    chunks(2 * STEPS + 2, give_sem, take_sem).wait_send()


def local(gradient, momentum, owners):
    layers, held, depth, width = gradient.shape
    slot_count = momentum.shape[1]
    fsdp_count = lax.axis_size("fsdp")
    rep_count = lax.axis_size("rep")
    vmem = pl.BlockSpec(memory_space=pltpu.VMEM)
    lanes = (fsdp_count, slot_count, depth, width)
    dma = pltpu.SemaphoreType.DMA
    update, momentum_new = pl.pallas_call(
        kernel,
        out_shape=(
            jax.ShapeDtypeStruct((layers, held * rep_count, depth, width), BF16),
            jax.ShapeDtypeStruct(momentum.shape, BF16),
        ),
        in_specs=[pl.BlockSpec(memory_space=pltpu.SMEM), vmem, vmem],
        out_specs=(vmem, vmem),
        scratch_shapes=[
            pltpu.VMEM(lanes, BF16),
            pltpu.VMEM(lanes, BF16),
            pltpu.VMEM(lanes, BF16),
            pltpu.VMEM(lanes, BF16),
            pltpu.VMEM((layers * held * depth, fsdp_count * slot_count * depth), BF16),
            dma, dma, dma, dma, dma,
            dma,
            dma((STEPS + 1, 2, PIECES)),
            dma, dma,
            dma((PIECES,)),
        ],
        compiler_params=pltpu.CompilerParams(
            collective_id=1, has_side_effects=True, vmem_limit_bytes=40 * 2**20),
        cost_estimate=pl.CostEstimate(flops=3 * 10**9, bytes_accessed=2**23, transcendentals=0),
    )(owners[:, :, 0], gradient, momentum)
    return (update, momentum_new)


def solution(mesh):
    placed = (P(None, "rep", "fsdp", None), P("rep", "fsdp", None, None), P("rep", None, None))
    return jax.shard_map(
        local,
        mesh=mesh,
        in_specs=placed,
        out_specs=(P(None, None, "fsdp", None), P("rep", "fsdp", None, None)),
        check_vma=False,
    )
```

```python
import functools
import math

import jax
import jax.numpy as jnp
from jax import lax
from jax.experimental import pallas as pl
from jax.experimental.pallas import tpu as pltpu
from jax.sharding import PartitionSpec as P

RANK = 512
BLOCK = 128
ROWS_Y = 8
ROWS_X = 4
CHIPS = 16
PIECES = 8
ITERS = 5
SURE = 4
STEPS = 10

beta_decay = 0.95
coef_a = 3.4445
coef_b = -4.775
coef_c = 2.0315
epsilon = 1e-07
muon_scale = 0.2 * math.sqrt(max(RANK, BLOCK))

F32 = jnp.float32
BF16 = jnp.bfloat16
MESH = pl.DeviceIdType.MESH
OFFSETS = sorted(
    [(y, x) for y in range(ROWS_Y) for x in range(ROWS_X) if (y, x) != (0, 0)],
    key=lambda o: -(min(o[0], ROWS_Y - o[0]) + min(o[1], ROWS_X - o[1])),
)


def split(value):
    high = value.astype(BF16)
    rest = value - high.astype(F32)
    mid = rest.astype(BF16)
    low = (rest - mid.astype(F32)).astype(BF16)
    return high, mid, low


def product(left, right):
    lh, lm, ll = left
    rh, rm, rl = right
    wide = jnp.concatenate([rh, rm], axis=1)
    main = jnp.dot(
        jnp.concatenate([lh, lm], axis=1), jnp.concatenate([wide, wide], axis=0), preferred_element_type=F32
    )
    rest = jnp.dot(
        jnp.concatenate([lh, ll], axis=1), jnp.concatenate([rl, rh], axis=0), preferred_element_type=F32
    )
    return main[:, :BLOCK] + (main[:, BLOCK:] + rest)


def gram(parts):
    high, mid, low = parts
    both = jnp.concatenate([high, mid], axis=1)
    dims = (((0,), (0,)), ((), ()))
    main = lax.dot_general(both, both, dims, preferred_element_type=F32)
    rest = lax.dot_general(high, low, dims, preferred_element_type=F32)
    cross = main[:BLOCK, BLOCK:] + main[BLOCK:, :BLOCK]
    return main[:BLOCK, :BLOCK] + (cross + (main[BLOCK:, BLOCK:] + (rest + rest.T)))


def orthogonalize(blends):
    row = lax.broadcasted_iota(jnp.int32, (BLOCK, BLOCK), 0)
    col = lax.broadcasted_iota(jnp.int32, (BLOCK, BLOCK), 1)
    eye = coef_a * (row == col).astype(F32)
    scales = [
        1.0 / (jnp.sqrt(jnp.sum(b * b, axis=(0, 1), keepdims=True)) + epsilon) for b in blends
    ]
    currents = blends
    for step in range(ITERS):
        parts = [split(y) for y in currents]
        grams = [gram(p) for p in parts]
        if step == 0:
            grams = [(g * v) * v for g, v in zip(grams, scales)]
        pieces = [split(g) for g in grams]
        squares = [product(p, p) for p in pieces]
        factors = [eye + coef_b * g + coef_c * s for g, s in zip(grams, squares)]
        if step == 0:
            factors = [f * v for f, v in zip(factors, scales)]
        currents = [product(p, split(f)) for p, f in zip(parts, factors)]
    return currents


def kernel(
    owner_hbm, gradient_hbm, momentum_hbm, update_ref, new_ref,
    owner_ref, gradient_ref, momentum_ref, packed, blocks, owned, returned, spread, load_sem,
    out_sem, in_sem, back_sem, home_sem, self_sem,
    go_sem, come_sem, give_sem, take_sem, first_sem,
):
    rep = lax.axis_index("rep")
    me = lax.axis_index("fsdp")
    core = lax.rem(rep, 2)
    chip = lax.div(rep, 2)
    way = 1 - 2 * core
    ahead = lax.rem(chip + way + CHIPS, CHIPS) * 2 + core
    behind = lax.rem(chip - way + CHIPS, CHIPS) * 2 + core
    twin = chip * 2 + 1 - core
    mine_y = lax.div(me, ROWS_X)
    mine_x = lax.rem(me, ROWS_X)
    fsdp_count, slot_count, depth, width = packed.shape
    layers, _, _, _ = gradient_ref.shape
    held = gradient_ref.shape[1]
    flat_rows = layers * held
    block_rows = flat_rows * depth
    slot_rows = fsdp_count * slot_count * depth

    def peer(offset):
        return lax.rem(mine_y + offset[0], ROWS_Y) * ROWS_X + lax.rem(mine_x + offset[1], ROWS_X)

    barrier = pltpu.get_barrier_semaphore()
    for offset in OFFSETS:
        pl.semaphore_signal(barrier, inc=1, device_id={"fsdp": peer(offset)}, device_id_type=MESH)
    for other in (ahead, behind, twin):
        pl.semaphore_signal(barrier, inc=1, device_id={"rep": other}, device_id_type=MESH)

    loads = [
        pltpu.make_async_copy(source, target, load_sem.at[i])
        for i, (source, target) in enumerate(
            [(owner_hbm, owner_ref), (gradient_hbm, gradient_ref), (momentum_hbm, momentum_ref)])
    ]
    for load in loads:
        load.start()
    loads[0].wait()

    names = [owner_ref[j % held, j // held] for j in range(flat_rows)]

    def targets(shape, dim):
        at = lax.broadcasted_iota(jnp.int32, shape, dim)
        number = at // depth
        owner = jnp.zeros(shape, jnp.int32)
        for j in range(flat_rows):
            owner = jnp.where(number == j, names[j], owner)
        slot = jnp.zeros(shape, jnp.int32)
        for j in range(flat_rows):
            slot += jnp.where((number > j) & (owner == names[j]), 1, 0)
        return (owner * slot_count + slot) * depth + lax.rem(at, depth)

    across = targets((1, block_rows), 1)
    place = (lax.broadcasted_iota(jnp.int32, (slot_rows, block_rows), 0) == across).astype(F32).astype(BF16)
    loads[1].wait()
    packed[...] = jnp.dot(
        place, gradient_ref[...].reshape(block_rows, width), preferred_element_type=F32
    ).astype(BF16).reshape(packed.shape)

    pl.semaphore_wait(barrier, len(OFFSETS) + 3)

    def swap(source, landing, sent, got, offset):
        other = peer(offset)
        return pltpu.make_async_remote_copy(
            src_ref=source.at[other], dst_ref=landing.at[me], send_sem=sent, recv_sem=got,
            device_id={"fsdp": other}, device_id_type=MESH)

    def exchange(source, landing, sent, got):
        for offset in OFFSETS:
            swap(source, landing, sent, got, offset).start()
        stays = pltpu.make_async_copy(source.at[me], landing.at[me], self_sem)
        stays.start()
        return stays

    def finish(landing, sent, got, stays):
        stays.wait()
        other = peer(OFFSETS[0])
        whole = landing.at[pl.ds(0, len(OFFSETS))]
        every = pltpu.make_async_remote_copy(
            src_ref=whole, dst_ref=whole, send_sem=sent, recv_sem=got,
            device_id={"fsdp": other}, device_id_type=MESH)
        every.wait_recv()
        every.wait_send()

    stays = exchange(packed, blocks, out_sem, in_sem)
    down = targets((block_rows, 1), 0)
    spread[...] = (lax.broadcasted_iota(jnp.int32, (block_rows, slot_rows), 1) == down).astype(F32).astype(BF16)
    finish(blocks, out_sem, in_sem, stays)

    loads[2].wait()
    blends = []
    for slot in range(slot_count):
        fresh = blocks[:, slot].reshape(RANK, width).astype(F32)
        carried = beta_decay * momentum_ref[0, slot].astype(F32) + fresh
        new_ref[0, slot] = carried.astype(BF16)
        blends.append(fresh + beta_decay * carried)
    for slot, current in enumerate(orthogonalize(blends)):
        owned[:, slot] = (muon_scale * current).astype(BF16).reshape(fsdp_count, depth, width)

    stays = exchange(owned, returned, back_sem, home_sem)
    finish(returned, back_sem, home_sem, stays)

    update_ref[:, pl.ds(rep * held, held)] = jnp.dot(
        spread[...], returned[...].reshape(slot_rows, width), preferred_element_type=F32
    ).astype(BF16).reshape(layers, held, depth, width)

    part = layers // PIECES

    def source(back, stream):
        return lax.rem(chip - back * (1 - 2 * stream) + 2 * CHIPS, CHIPS)

    def reach(from_chip, other, stream):
        long = (from_chip >= 8) & (from_chip <= 10)
        return jnp.where(long, jnp.where(stream == 1, from_chip, CHIPS - 1 - from_chip), 8 - other)

    def comes(step, other, stream):
        return step + 1 <= reach(source(step + 1, stream), other, stream)

    def goes_on(step, other):
        return step + 2 <= reach(source(step + 1, core), other, core)

    def chunk(back, other):
        return source(back, core) * 2 + (core if other == 0 else 1 - core)

    def where(number, piece):
        return update_ref.at[pl.ds(piece * part, part), pl.ds(number * held, held)]

    def hop(step, other, piece):
        at = where(chunk(step, other), piece)
        return pltpu.make_async_remote_copy(
            src_ref=at, dst_ref=at, send_sem=go_sem.at[step, other], recv_sem=come_sem.at[step, other, piece],
            device_id={"rep": ahead}, device_id_type=MESH)

    def share(number, piece, sent, got):
        at = where(number, piece)
        return pltpu.make_async_remote_copy(
            src_ref=at, dst_ref=at, send_sem=sent, recv_sem=got,
            device_id={"rep": twin}, device_id_type=MESH)

    def pass_on(step, other, piece):
        share(chunk(step + 1, other), piece, give_sem.at[step, other], take_sem.at[step, other]).start()

    for piece in range(PIECES):
        share(rep, piece, self_sem, first_sem.at[piece]).start()
        hop(0, 0, piece).start()
    for piece in range(PIECES):
        share(rep, piece, self_sem, first_sem.at[piece]).wait_recv()
        hop(0, 1, piece).start()

    @pl.loop(0, SURE)
    def _(step):
        for other in range(2):
            for piece in range(PIECES):
                hop(step, other, piece).wait_recv()
                hop(step + 1, other, piece).start()
                pass_on(step, other, piece)

    @pl.loop(SURE, STEPS)
    def _(step):
        for other in range(2):
            @pl.when(goes_on(step, other))
            def _():
                for piece in range(PIECES):
                    hop(step, other, piece).wait_recv()
                    hop(step + 1, other, piece).start()
                    pass_on(step, other, piece)

            @pl.when(comes(step, other, core) & jnp.logical_not(goes_on(step, other)))
            def _():
                for piece in range(PIECES):
                    hop(step, other, piece).wait_recv()
                    pass_on(step, other, piece)

    def whole(sent, got):
        some = update_ref.at[:, pl.ds(rep * held, held)]
        return pltpu.make_async_remote_copy(
            src_ref=some, dst_ref=some, send_sem=sent, recv_sem=got,
            device_id={"rep": twin}, device_id_type=MESH)

    whole(self_sem, self_sem).wait_send()
    for other in range(2):
        whole(go_sem.at[0, other], self_sem).wait_send()

    @pl.loop(0, STEPS)
    def _(step):
        for other in range(2):
            @pl.when(comes(step, other, core))
            def _():
                whole(give_sem.at[step, other], self_sem).wait_send()

            @pl.when(goes_on(step, other))
            def _():
                whole(go_sem.at[step + 1, other], self_sem).wait_send()

            @pl.when(comes(step, other, 1 - core))
            def _():
                whole(self_sem, take_sem.at[step, other]).wait_recv()


def store_kernel(update_ref, new_ref, update_hbm, new_hbm, sems):
    copies = [
        pltpu.make_async_copy(update_ref, update_hbm, sems.at[0]),
        pltpu.make_async_copy(new_ref, new_hbm, sems.at[1]),
    ]
    for copy in copies:
        copy.start()
    for copy in copies:
        copy.wait()


def local(gradient, momentum, owners):
    layers, held, depth, width = gradient.shape
    slot_count = momentum.shape[1]
    fsdp_count = lax.axis_size("fsdp")
    rep_count = lax.axis_size("rep")
    vmem = pl.BlockSpec(memory_space=pltpu.VMEM)
    hbm = pl.BlockSpec(memory_space=pltpu.HBM)
    lanes = (fsdp_count, slot_count, depth, width)
    dma = pltpu.SemaphoreType.DMA
    update, momentum_new = pl.pallas_call(
        kernel,
        out_shape=(
            jax.ShapeDtypeStruct((layers, held * rep_count, depth, width), BF16),
            jax.ShapeDtypeStruct(momentum.shape, BF16),
        ),
        in_specs=[hbm, hbm, hbm],
        out_specs=(vmem, vmem),
        scratch_shapes=[
            pltpu.SMEM((held, layers), jnp.int32),
            pltpu.VMEM(gradient.shape, BF16),
            pltpu.VMEM(momentum.shape, BF16),
            pltpu.VMEM(lanes, BF16),
            pltpu.VMEM(lanes, BF16),
            pltpu.VMEM(lanes, BF16),
            pltpu.VMEM(lanes, BF16),
            pltpu.VMEM((layers * held * depth, fsdp_count * slot_count * depth), BF16),
            dma((3,)),
            dma, dma, dma, dma, dma,
            dma((STEPS + 1, 2)),
            dma((STEPS + 1, 2, PIECES)),
            dma((STEPS, 2)), dma((STEPS + 1, 2)),
            dma((PIECES,)),
        ],
        compiler_params=pltpu.CompilerParams(
            collective_id=1, has_side_effects=True, vmem_limit_bytes=40 * 2**20),
        cost_estimate=pl.CostEstimate(flops=3 * 10**9, bytes_accessed=2**23, transcendentals=0),
    )(*(pltpu.with_memory_space_constraint(a, pltpu.HBM) for a in (owners[:, :, 0], gradient, momentum)))
    return pl.pallas_call(
        store_kernel,
        out_shape=(
            jax.ShapeDtypeStruct(update.shape, BF16),
            jax.ShapeDtypeStruct(momentum_new.shape, BF16),
        ),
        in_specs=[vmem, vmem],
        out_specs=(hbm, hbm),
        scratch_shapes=[dma((2,))],
        compiler_params=pltpu.CompilerParams(vmem_limit_bytes=16 * 2**20),
    )(update, momentum_new)


def solution(mesh):
    placed = (P(None, "rep", "fsdp", None), P("rep", "fsdp", None, None), P("rep", None, None))
    return jax.shard_map(
        local,
        mesh=mesh,
        in_specs=placed,
        out_specs=(P(None, None, "fsdp", None), P("rep", "fsdp", None, None)),
        check_vma=False,
    )
```

```python
import functools
import math

import jax
import jax.numpy as jnp
from jax import lax
from jax.experimental import pallas as pl
from jax.experimental.pallas import tpu as pltpu
from jax.sharding import PartitionSpec as P

RANK = 512
BLOCK = 128
ROWS_Y = 8
ROWS_X = 4
CHIPS = 16
PIECES = 8
ITERS = 5
LAG = 6

beta_decay = 0.95
coef_a = 3.4445
coef_b = -4.775
coef_c = 2.0315
epsilon = 1e-07
muon_scale = 0.2 * math.sqrt(max(RANK, BLOCK))

F32 = jnp.float32
BF16 = jnp.bfloat16
MESH = pl.DeviceIdType.MESH
OFFSETS = sorted(
    [(y, x) for y in range(ROWS_Y) for x in range(ROWS_X) if (y, x) != (0, 0)],
    key=lambda o: -(min(o[0], ROWS_Y - o[0]) + min(o[1], ROWS_X - o[1])),
)


DOWN = [[7, 8] for _ in range(CHIPS)]
DOWN[8:14] = [[8, 8], [9, 9], [9, 10], [9, 9], [8, 9], [9, 9]]


def arrivals(chip, stream):
    items = []
    for back in range(1, CHIPS):
        start = (chip - back) % CHIPS if stream == 0 else (chip + back) % CHIPS
        for other in range(2):
            reach = DOWN[start][(stream + other) % 2]
            if back <= (reach if stream == 1 else CHIPS - 1 - reach):
                items.append(2 * (back - 1) + other)
    return items


COUNTS = [[len(arrivals(chip, stream)) for chip in range(CHIPS)] for stream in range(2)]
ITEMS = max(map(max, COUNTS))
for number_of in range(CHIPS):
    for stream_of in range(2):
        onto = COUNTS[stream_of][(number_of + 1 - 2 * stream_of) % CHIPS]
        assert arrivals(number_of, stream_of) == list(range(COUNTS[stream_of][number_of]))
        assert LAG <= onto - 2 <= COUNTS[stream_of][number_of]
    assert COUNTS[0][number_of] + COUNTS[1][number_of] == 2 * (CHIPS - 1)


def look_up(first, second, chip, core):
    found = jnp.where(core == 0, first[0], second[0])
    for at in range(1, CHIPS):
        found = jnp.where(chip == at, jnp.where(core == 0, first[at], second[at]), found)
    return found


def split(value):
    high = value.astype(BF16)
    rest = value - high.astype(F32)
    mid = rest.astype(BF16)
    low = (rest - mid.astype(F32)).astype(BF16)
    return high, mid, low


def product(left, right):
    lh, lm, ll = left
    rh, rm, rl = right
    wide = jnp.concatenate([rh, rm], axis=1)
    main = jnp.dot(
        jnp.concatenate([lh, lm], axis=1), jnp.concatenate([wide, wide], axis=0), preferred_element_type=F32
    )
    rest = jnp.dot(
        jnp.concatenate([lh, ll], axis=1), jnp.concatenate([rl, rh], axis=0), preferred_element_type=F32
    )
    return main[:, :BLOCK] + (main[:, BLOCK:] + rest)


def gram(parts):
    high, mid, low = parts
    both = jnp.concatenate([high, mid], axis=1)
    dims = (((0,), (0,)), ((), ()))
    main = lax.dot_general(both, both, dims, preferred_element_type=F32)
    rest = lax.dot_general(high, low, dims, preferred_element_type=F32)
    cross = main[:BLOCK, BLOCK:] + main[BLOCK:, :BLOCK]
    return main[:BLOCK, :BLOCK] + (cross + (main[BLOCK:, BLOCK:] + (rest + rest.T)))


def orthogonalize(blends):
    row = lax.broadcasted_iota(jnp.int32, (BLOCK, BLOCK), 0)
    col = lax.broadcasted_iota(jnp.int32, (BLOCK, BLOCK), 1)
    eye = coef_a * (row == col).astype(F32)
    scales = [
        1.0 / (jnp.sqrt(jnp.sum(b * b, axis=(0, 1), keepdims=True)) + epsilon) for b in blends
    ]
    currents = blends
    for step in range(ITERS):
        parts = [split(y) for y in currents]
        grams = [gram(p) for p in parts]
        if step == 0:
            grams = [(g * v) * v for g, v in zip(grams, scales)]
        pieces = [split(g) for g in grams]
        squares = [product(p, p) for p in pieces]
        factors = [eye + coef_b * g + coef_c * s for g, s in zip(grams, squares)]
        if step == 0:
            factors = [f * v for f, v in zip(factors, scales)]
        currents = [product(p, split(f)) for p, f in zip(parts, factors)]
    return currents


def kernel(
    owner_hbm, gradient_hbm, momentum_hbm, update_ref, new_ref,
    owner_ref, gradient_ref, momentum_ref, packed, blocks, owned, returned, spread, load_sem,
    out_sem, in_sem, back_sem, home_sem, self_sem,
    go_sem, come_sem, give_sem, take_sem, first_sem,
):
    rep = lax.axis_index("rep")
    me = lax.axis_index("fsdp")
    core = lax.rem(rep, 2)
    chip = lax.div(rep, 2)
    way = 1 - 2 * core
    ahead = lax.rem(chip + way + CHIPS, CHIPS) * 2 + core
    behind = lax.rem(chip - way + CHIPS, CHIPS) * 2 + core
    twin = chip * 2 + 1 - core
    mine_y = lax.div(me, ROWS_X)
    mine_x = lax.rem(me, ROWS_X)
    fsdp_count, slot_count, depth, width = packed.shape
    layers, _, _, _ = gradient_ref.shape
    held = gradient_ref.shape[1]
    flat_rows = layers * held
    block_rows = flat_rows * depth
    slot_rows = fsdp_count * slot_count * depth

    def peer(offset):
        return lax.rem(mine_y + offset[0], ROWS_Y) * ROWS_X + lax.rem(mine_x + offset[1], ROWS_X)

    barrier = pltpu.get_barrier_semaphore()
    for offset in OFFSETS:
        pl.semaphore_signal(barrier, inc=1, device_id={"fsdp": peer(offset)}, device_id_type=MESH)
    for other in (ahead, behind, twin):
        pl.semaphore_signal(barrier, inc=1, device_id={"rep": other}, device_id_type=MESH)

    loads = [
        pltpu.make_async_copy(source, target, load_sem.at[i])
        for i, (source, target) in enumerate(
            [(owner_hbm, owner_ref), (gradient_hbm, gradient_ref), (momentum_hbm, momentum_ref)])
    ]
    for load in loads:
        load.start()
    loads[0].wait()

    names = [owner_ref[j % held, j // held] for j in range(flat_rows)]

    def targets(shape, dim):
        at = lax.broadcasted_iota(jnp.int32, shape, dim)
        number = at // depth
        owner = jnp.zeros(shape, jnp.int32)
        for j in range(flat_rows):
            owner = jnp.where(number == j, names[j], owner)
        slot = jnp.zeros(shape, jnp.int32)
        for j in range(flat_rows):
            slot += jnp.where((number > j) & (owner == names[j]), 1, 0)
        return (owner * slot_count + slot) * depth + lax.rem(at, depth)

    across = targets((1, block_rows), 1)
    place = (lax.broadcasted_iota(jnp.int32, (slot_rows, block_rows), 0) == across).astype(F32).astype(BF16)
    loads[1].wait()
    packed[...] = jnp.dot(
        place, gradient_ref[...].reshape(block_rows, width), preferred_element_type=F32
    ).astype(BF16).reshape(packed.shape)

    pl.semaphore_wait(barrier, len(OFFSETS) + 3)

    def swap(source, landing, sent, got, offset):
        other = peer(offset)
        return pltpu.make_async_remote_copy(
            src_ref=source.at[other], dst_ref=landing.at[me], send_sem=sent, recv_sem=got,
            device_id={"fsdp": other}, device_id_type=MESH)

    def exchange(source, landing, sent, got):
        for offset in OFFSETS:
            swap(source, landing, sent, got, offset).start()
        stays = pltpu.make_async_copy(source.at[me], landing.at[me], self_sem)
        stays.start()
        return stays

    def exchanged(landing, sent, got):
        every = landing.at[pl.ds(0, len(OFFSETS))]
        return pltpu.make_async_remote_copy(
            src_ref=every, dst_ref=every, send_sem=sent, recv_sem=got,
            device_id={"fsdp": peer(OFFSETS[0])}, device_id_type=MESH)

    def finish(landing, sent, got, stays):
        stays.wait()
        exchanged(landing, sent, got).wait_recv()

    stays = exchange(packed, blocks, out_sem, in_sem)
    down = targets((block_rows, 1), 0)
    spread[...] = (lax.broadcasted_iota(jnp.int32, (block_rows, slot_rows), 1) == down).astype(F32).astype(BF16)
    finish(blocks, out_sem, in_sem, stays)

    loads[2].wait()
    blends = []
    for slot in range(slot_count):
        fresh = blocks[:, slot].reshape(RANK, width).astype(F32)
        carried = beta_decay * momentum_ref[0, slot].astype(F32) + fresh
        blends.append(fresh + beta_decay * carried)
    for slot, current in enumerate(orthogonalize(blends)):
        owned[:, slot] = (muon_scale * current).astype(BF16).reshape(fsdp_count, depth, width)

    stays = exchange(owned, returned, back_sem, home_sem)
    for slot in range(slot_count):
        fresh = blocks[:, slot].reshape(RANK, width).astype(F32)
        carried = beta_decay * momentum_ref[0, slot].astype(F32) + fresh
        new_ref[0, slot] = carried.astype(BF16)
    finish(returned, back_sem, home_sem, stays)

    update_ref[:, pl.ds(rep * held, held)] = jnp.dot(
        spread[...], returned[...].reshape(slot_rows, width), preferred_element_type=F32
    ).astype(BF16).reshape(layers, held, depth, width)

    part = layers // PIECES
    count = look_up(COUNTS[0], COUNTS[1], chip, core)
    ahead_count = look_up(COUNTS[0][1:] + COUNTS[0][:1], COUNTS[1][-1:] + COUNTS[1][:-1], chip, core)
    onward = ahead_count - 2

    def number(item):
        from_chip = lax.rem(chip - (lax.div(item, 2) + 1) * way + 2 * CHIPS, CHIPS)
        return from_chip * 2 + lax.rem(core + item, 2)

    def where(chunk, piece):
        return update_ref.at[pl.ds(piece * part, part), pl.ds(chunk * held, held)]

    def hop(item, at, piece):
        return pltpu.make_async_remote_copy(
            src_ref=at, dst_ref=at, send_sem=go_sem.at[item], recv_sem=come_sem.at[item, piece],
            device_id={"rep": ahead}, device_id_type=MESH)

    def share(at, sent, got):
        return pltpu.make_async_remote_copy(
            src_ref=at, dst_ref=at, send_sem=sent, recv_sem=got,
            device_id={"rep": twin}, device_id_type=MESH)

    for piece in range(PIECES):
        share(where(rep, piece), self_sem, first_sem.at[piece]).start()
        hop(0, where(rep, piece), piece).start()
    for piece in range(PIECES):
        at = where(chip * 2 + 1 - core, piece)
        share(at, self_sem, first_sem.at[piece]).wait_recv()
        hop(1, at, piece).start()

    whole = update_ref.at[:, pl.ds(rep * held, held)]

    @pl.loop(0, onward)
    def _(item):
        chunk = number(item)
        for piece in range(PIECES):
            at = where(chunk, piece)
            hop(item, at, piece).wait_recv()
            hop(item + 2, at, piece).start()
            share(at, give_sem.at[item], take_sem.at[item]).start()

        @pl.when(item >= LAG)
        def _():
            share(whole, go_sem.at[item - LAG], self_sem).wait_send()
            share(whole, give_sem.at[item - LAG], self_sem).wait_send()

    @pl.loop(onward, count)
    def _(item):
        chunk = number(item)
        for piece in range(PIECES):
            at = where(chunk, piece)
            hop(item, at, piece).wait_recv()
            share(at, give_sem.at[item], take_sem.at[item]).start()

    share(whole, self_sem, self_sem).wait_send()
    for sem in (out_sem, back_sem):
        exchanged(packed, sem, sem).wait_send()

    @pl.loop(onward - LAG, ahead_count)
    def _(item):
        share(whole, go_sem.at[item], self_sem).wait_send()

    @pl.loop(onward - LAG, count)
    def _(item):
        share(whole, give_sem.at[item], self_sem).wait_send()

    @pl.loop(0, 2 * (CHIPS - 1) - count)
    def _(item):
        share(whole, self_sem, take_sem.at[item]).wait_recv()


def store_kernel(update_ref, new_ref, update_hbm, new_hbm, sems):
    copies = [
        pltpu.make_async_copy(update_ref, update_hbm, sems.at[0]),
        pltpu.make_async_copy(new_ref, new_hbm, sems.at[1]),
    ]
    for copy in copies:
        copy.start()
    for copy in copies:
        copy.wait()


def local(gradient, momentum, owners):
    layers, held, depth, width = gradient.shape
    slot_count = momentum.shape[1]
    fsdp_count = lax.axis_size("fsdp")
    rep_count = lax.axis_size("rep")
    vmem = pl.BlockSpec(memory_space=pltpu.VMEM)
    hbm = pl.BlockSpec(memory_space=pltpu.HBM)
    lanes = (fsdp_count, slot_count, depth, width)
    dma = pltpu.SemaphoreType.DMA
    update, momentum_new = pl.pallas_call(
        kernel,
        out_shape=(
            jax.ShapeDtypeStruct((layers, held * rep_count, depth, width), BF16),
            jax.ShapeDtypeStruct(momentum.shape, BF16),
        ),
        in_specs=[hbm, hbm, hbm],
        out_specs=(vmem, vmem),
        scratch_shapes=[
            pltpu.SMEM((held, layers), jnp.int32),
            pltpu.VMEM(gradient.shape, BF16),
            pltpu.VMEM(momentum.shape, BF16),
            pltpu.VMEM(lanes, BF16),
            pltpu.VMEM(lanes, BF16),
            pltpu.VMEM(lanes, BF16),
            pltpu.VMEM(lanes, BF16),
            pltpu.VMEM((layers * held * depth, fsdp_count * slot_count * depth), BF16),
            dma((3,)),
            dma, dma, dma, dma, dma,
            dma((ITEMS,)),
            dma((ITEMS, PIECES)),
            dma((ITEMS,)), dma((ITEMS,)),
            dma((PIECES,)),
        ],
        compiler_params=pltpu.CompilerParams(
            collective_id=1, has_side_effects=True, vmem_limit_bytes=40 * 2**20),
        cost_estimate=pl.CostEstimate(flops=3 * 10**9, bytes_accessed=2**23, transcendentals=0),
    )(*(pltpu.with_memory_space_constraint(a, pltpu.HBM) for a in (owners[:, :, 0], gradient, momentum)))
    return pl.pallas_call(
        store_kernel,
        out_shape=(
            jax.ShapeDtypeStruct(update.shape, BF16),
            jax.ShapeDtypeStruct(momentum_new.shape, BF16),
        ),
        in_specs=[vmem, vmem],
        out_specs=(hbm, hbm),
        scratch_shapes=[dma((2,))],
        compiler_params=pltpu.CompilerParams(vmem_limit_bytes=16 * 2**20),
    )(update, momentum_new)


def solution(mesh):
    placed = (P(None, "rep", "fsdp", None), P("rep", "fsdp", None, None), P("rep", None, None))
    return jax.shard_map(
        local,
        mesh=mesh,
        in_specs=placed,
        out_specs=(P(None, None, "fsdp", None), P("rep", "fsdp", None, None)),
        check_vma=False,
    )
```

```python
import functools
import math

import jax
import jax.numpy as jnp
from jax import lax
from jax.experimental import pallas as pl
from jax.experimental.pallas import tpu as pltpu
from jax.sharding import PartitionSpec as P

RANK = 512
BLOCK = 128
ROWS_Y = 8
ROWS_X = 4
CHIPS = 16
PIECES = 8
ITERS = 5
LAG = 6

beta_decay = 0.95
coef_a = 3.4445
coef_b = -4.775
coef_c = 2.0315
epsilon = 1e-07
muon_scale = 0.2 * math.sqrt(max(RANK, BLOCK))

F32 = jnp.float32
BF16 = jnp.bfloat16
MESH = pl.DeviceIdType.MESH
OFFSETS = sorted(
    [(y, x) for y in range(ROWS_Y) for x in range(ROWS_X) if (y, x) != (0, 0)],
    key=lambda o: -(min(o[0], ROWS_Y - o[0]) + min(o[1], ROWS_X - o[1])),
)


DOWN = [7 + chip % 2 for chip in range(CHIPS)]
DOWN[8:14] = [8, 9, 9, 9, 8, 9]


def arrivals(chip, stream):
    found = []
    for back in range(1, CHIPS):
        start = (chip - back) % CHIPS if stream == 0 else (chip + back) % CHIPS
        if back <= (DOWN[start] if stream == 1 else CHIPS - 1 - DOWN[start]):
            found.append(back)
    return found


COUNTS = [[2 * len(arrivals(chip, stream)) for chip in range(CHIPS)] for stream in range(2)]
ITEMS = max(map(max, COUNTS))
for number_of in range(CHIPS):
    for stream_of in range(2):
        onto = COUNTS[stream_of][(number_of + 1 - 2 * stream_of) % CHIPS]
        assert arrivals(number_of, stream_of) == list(range(1, COUNTS[stream_of][number_of] // 2 + 1))
        assert LAG <= onto - 2 <= COUNTS[stream_of][number_of]
    assert COUNTS[0][number_of] + COUNTS[1][number_of] == 2 * (CHIPS - 1)


def look_up(first, second, chip, core):
    found = jnp.where(core == 0, first[0], second[0])
    for at in range(1, CHIPS):
        found = jnp.where(chip == at, jnp.where(core == 0, first[at], second[at]), found)
    return found


def split(value):
    high = value.astype(BF16)
    rest = value - high.astype(F32)
    mid = rest.astype(BF16)
    low = (rest - mid.astype(F32)).astype(BF16)
    return high, mid, low


def product(left, right):
    lh, lm, ll = left
    rh, rm, rl = right
    wide = jnp.concatenate([rh, rm], axis=1)
    main = jnp.dot(
        jnp.concatenate([lh, lm], axis=1), jnp.concatenate([wide, wide], axis=0), preferred_element_type=F32
    )
    rest = jnp.dot(
        jnp.concatenate([lh, ll], axis=1), jnp.concatenate([rl, rh], axis=0), preferred_element_type=F32
    )
    return main[:, :BLOCK] + (main[:, BLOCK:] + rest)


def gram(parts):
    high, mid, low = parts
    both = jnp.concatenate([high, mid], axis=1)
    dims = (((0,), (0,)), ((), ()))
    main = lax.dot_general(both, both, dims, preferred_element_type=F32)
    rest = lax.dot_general(high, low, dims, preferred_element_type=F32)
    cross = main[:BLOCK, BLOCK:] + main[BLOCK:, :BLOCK]
    return main[:BLOCK, :BLOCK] + (cross + (main[BLOCK:, BLOCK:] + (rest + rest.T)))


def orthogonalize(blends):
    row = lax.broadcasted_iota(jnp.int32, (BLOCK, BLOCK), 0)
    col = lax.broadcasted_iota(jnp.int32, (BLOCK, BLOCK), 1)
    eye = coef_a * (row == col).astype(F32)
    scales = [
        1.0 / (jnp.sqrt(jnp.sum(b * b, axis=(0, 1), keepdims=True)) + epsilon) for b in blends
    ]
    currents = blends
    for step in range(ITERS):
        parts = [split(y) for y in currents]
        grams = [gram(p) for p in parts]
        if step == 0:
            grams = [(g * v) * v for g, v in zip(grams, scales)]
        pieces = [split(g) for g in grams]
        squares = [product(p, p) for p in pieces]
        factors = [eye + coef_b * g + coef_c * s for g, s in zip(grams, squares)]
        if step == 0:
            factors = [f * v for f, v in zip(factors, scales)]
        currents = [product(p, split(f)) for p, f in zip(parts, factors)]
    return currents


def kernel(
    owner_hbm, gradient_hbm, momentum_hbm, update_ref, new_ref,
    owner_ref, gradient_ref, momentum_ref, packed, blocks, owned, returned, spread, load_sem,
    out_sem, in_sem, back_sem, home_sem, self_sem,
    go_sem, come_sem, give_sem, take_sem, first_sem,
):
    rep = lax.axis_index("rep")
    me = lax.axis_index("fsdp")
    core = lax.rem(rep, 2)
    chip = lax.div(rep, 2)
    way = 1 - 2 * core
    ahead = lax.rem(chip + way + CHIPS, CHIPS) * 2 + core
    behind = lax.rem(chip - way + CHIPS, CHIPS) * 2 + core
    twin = chip * 2 + 1 - core
    cross = lax.rem(chip - way + CHIPS, CHIPS) * 2 + 1 - core
    mine_y = lax.div(me, ROWS_X)
    mine_x = lax.rem(me, ROWS_X)
    fsdp_count, slot_count, depth, width = packed.shape
    layers, _, _, _ = gradient_ref.shape
    held = gradient_ref.shape[1]
    flat_rows = layers * held
    block_rows = flat_rows * depth
    slot_rows = fsdp_count * slot_count * depth

    def peer(offset):
        return lax.rem(mine_y + offset[0], ROWS_Y) * ROWS_X + lax.rem(mine_x + offset[1], ROWS_X)

    barrier = pltpu.get_barrier_semaphore()
    for offset in OFFSETS:
        pl.semaphore_signal(barrier, inc=1, device_id={"fsdp": peer(offset)}, device_id_type=MESH)
    for other in (ahead, behind, twin, cross):
        pl.semaphore_signal(barrier, inc=1, device_id={"rep": other}, device_id_type=MESH)

    loads = [
        pltpu.make_async_copy(source, target, load_sem.at[i])
        for i, (source, target) in enumerate(
            [(owner_hbm, owner_ref), (gradient_hbm, gradient_ref), (momentum_hbm, momentum_ref)])
    ]
    for load in loads:
        load.start()
    loads[0].wait()

    names = [owner_ref[j % held, j // held] for j in range(flat_rows)]

    def targets(shape, dim):
        at = lax.broadcasted_iota(jnp.int32, shape, dim)
        number = at // depth
        owner = jnp.zeros(shape, jnp.int32)
        for j in range(flat_rows):
            owner = jnp.where(number == j, names[j], owner)
        slot = jnp.zeros(shape, jnp.int32)
        for j in range(flat_rows):
            slot += jnp.where((number > j) & (owner == names[j]), 1, 0)
        return (owner * slot_count + slot) * depth + lax.rem(at, depth)

    across = targets((1, block_rows), 1)
    place = (lax.broadcasted_iota(jnp.int32, (slot_rows, block_rows), 0) == across).astype(F32).astype(BF16)
    loads[1].wait()
    packed[...] = jnp.dot(
        place, gradient_ref[...].reshape(block_rows, width), preferred_element_type=F32
    ).astype(BF16).reshape(packed.shape)

    pl.semaphore_wait(barrier, len(OFFSETS) + 4)

    def swap(source, landing, sent, got, offset):
        other = peer(offset)
        return pltpu.make_async_remote_copy(
            src_ref=source.at[other], dst_ref=landing.at[me], send_sem=sent, recv_sem=got,
            device_id={"fsdp": other}, device_id_type=MESH)

    def exchange(source, landing, sent, got):
        for offset in OFFSETS:
            swap(source, landing, sent, got, offset).start()
        stays = pltpu.make_async_copy(source.at[me], landing.at[me], self_sem)
        stays.start()
        return stays

    def exchanged(landing, sent, got):
        every = landing.at[pl.ds(0, len(OFFSETS))]
        return pltpu.make_async_remote_copy(
            src_ref=every, dst_ref=every, send_sem=sent, recv_sem=got,
            device_id={"fsdp": peer(OFFSETS[0])}, device_id_type=MESH)

    def finish(landing, sent, got, stays):
        stays.wait()
        exchanged(landing, sent, got).wait_recv()

    stays = exchange(packed, blocks, out_sem, in_sem)
    down = targets((block_rows, 1), 0)
    spread[...] = (lax.broadcasted_iota(jnp.int32, (block_rows, slot_rows), 1) == down).astype(F32).astype(BF16)
    finish(blocks, out_sem, in_sem, stays)

    loads[2].wait()
    blends = []
    for slot in range(slot_count):
        fresh = blocks[:, slot].reshape(RANK, width).astype(F32)
        carried = beta_decay * momentum_ref[0, slot].astype(F32) + fresh
        blends.append(fresh + beta_decay * carried)
    for slot, current in enumerate(orthogonalize(blends)):
        owned[:, slot] = (muon_scale * current).astype(BF16).reshape(fsdp_count, depth, width)

    stays = exchange(owned, returned, back_sem, home_sem)
    for slot in range(slot_count):
        fresh = blocks[:, slot].reshape(RANK, width).astype(F32)
        carried = beta_decay * momentum_ref[0, slot].astype(F32) + fresh
        new_ref[0, slot] = carried.astype(BF16)
    finish(returned, back_sem, home_sem, stays)

    update_ref[:, pl.ds(rep * held, held)] = jnp.dot(
        spread[...], returned[...].reshape(slot_rows, width), preferred_element_type=F32
    ).astype(BF16).reshape(layers, held, depth, width)

    part = layers // PIECES
    count = look_up(COUNTS[0], COUNTS[1], chip, core)
    ahead_count = look_up(COUNTS[0][1:] + COUNTS[0][:1], COUNTS[1][-1:] + COUNTS[1][:-1], chip, core)
    onward = ahead_count - 2

    def number(item):
        from_chip = lax.rem(chip - (lax.div(item, 2) + 1) * way + 2 * CHIPS, CHIPS)
        return from_chip * 2 + 1 - lax.rem(item, 2)

    def where(chunk, piece):
        return update_ref.at[pl.ds(piece * part, part), pl.ds(chunk * held, held)]

    def hop(item, at, piece):
        return pltpu.make_async_remote_copy(
            src_ref=at, dst_ref=at, send_sem=go_sem.at[item], recv_sem=come_sem.at[item, piece],
            device_id={"rep": ahead}, device_id_type=MESH)

    def share(at, sent, got):
        return pltpu.make_async_remote_copy(
            src_ref=at, dst_ref=at, send_sem=sent, recv_sem=got,
            device_id={"rep": twin}, device_id_type=MESH)

    for piece in range(PIECES):
        at = where(rep, piece)
        for sem, target in ((0, ahead), (1, cross)):
            pltpu.make_async_remote_copy(
                src_ref=at, dst_ref=at, send_sem=go_sem.at[sem], recv_sem=come_sem.at[1 - core, piece],
                device_id={"rep": target}, device_id_type=MESH).start()
    for piece in range(PIECES):
        share(where(rep, piece), self_sem, first_sem).start()

    whole = update_ref.at[:, pl.ds(rep * held, held)]

    @pl.loop(0, onward)
    def _(item):
        chunk = number(item)
        for piece in range(PIECES):
            at = where(chunk, piece)
            hop(item, at, piece).wait_recv()
            hop(item + 2, at, piece).start()
            share(at, give_sem.at[item], take_sem.at[item]).start()

        @pl.when(item >= LAG)
        def _():
            share(whole, go_sem.at[item - LAG], self_sem).wait_send()
            share(whole, give_sem.at[item - LAG], self_sem).wait_send()

    @pl.loop(onward, count)
    def _(item):
        chunk = number(item)
        for piece in range(PIECES):
            at = where(chunk, piece)
            hop(item, at, piece).wait_recv()
            share(at, give_sem.at[item], take_sem.at[item]).start()

    share(whole, self_sem, first_sem).wait()
    for sem in (out_sem, back_sem):
        exchanged(packed, sem, sem).wait_send()

    @pl.loop(onward - LAG, ahead_count)
    def _(item):
        share(whole, go_sem.at[item], self_sem).wait_send()

    @pl.loop(onward - LAG, count)
    def _(item):
        share(whole, give_sem.at[item], self_sem).wait_send()

    @pl.loop(0, 2 * (CHIPS - 1) - count)
    def _(item):
        share(whole, self_sem, take_sem.at[item]).wait_recv()


def store_kernel(update_ref, new_ref, update_hbm, new_hbm, sems):
    copies = [
        pltpu.make_async_copy(update_ref, update_hbm, sems.at[0]),
        pltpu.make_async_copy(new_ref, new_hbm, sems.at[1]),
    ]
    for copy in copies:
        copy.start()
    for copy in copies:
        copy.wait()


def local(gradient, momentum, owners):
    layers, held, depth, width = gradient.shape
    slot_count = momentum.shape[1]
    fsdp_count = lax.axis_size("fsdp")
    rep_count = lax.axis_size("rep")
    vmem = pl.BlockSpec(memory_space=pltpu.VMEM)
    hbm = pl.BlockSpec(memory_space=pltpu.HBM)
    lanes = (fsdp_count, slot_count, depth, width)
    dma = pltpu.SemaphoreType.DMA
    update, momentum_new = pl.pallas_call(
        kernel,
        out_shape=(
            jax.ShapeDtypeStruct((layers, held * rep_count, depth, width), BF16),
            jax.ShapeDtypeStruct(momentum.shape, BF16),
        ),
        in_specs=[hbm, hbm, hbm],
        out_specs=(vmem, vmem),
        scratch_shapes=[
            pltpu.SMEM((held, layers), jnp.int32),
            pltpu.VMEM(gradient.shape, BF16),
            pltpu.VMEM(momentum.shape, BF16),
            pltpu.VMEM(lanes, BF16),
            pltpu.VMEM(lanes, BF16),
            pltpu.VMEM(lanes, BF16),
            pltpu.VMEM(lanes, BF16),
            pltpu.VMEM((layers * held * depth, fsdp_count * slot_count * depth), BF16),
            dma((3,)),
            dma, dma, dma, dma, dma,
            dma((ITEMS,)),
            dma((ITEMS, PIECES)),
            dma((ITEMS,)), dma((ITEMS,)),
            dma,
        ],
        compiler_params=pltpu.CompilerParams(
            collective_id=1, has_side_effects=True, vmem_limit_bytes=40 * 2**20),
        cost_estimate=pl.CostEstimate(flops=3 * 10**9, bytes_accessed=2**23, transcendentals=0),
    )(*(pltpu.with_memory_space_constraint(a, pltpu.HBM) for a in (owners[:, :, 0], gradient, momentum)))
    return pl.pallas_call(
        store_kernel,
        out_shape=(
            jax.ShapeDtypeStruct(update.shape, BF16),
            jax.ShapeDtypeStruct(momentum_new.shape, BF16),
        ),
        in_specs=[vmem, vmem],
        out_specs=(hbm, hbm),
        scratch_shapes=[dma((2,))],
        compiler_params=pltpu.CompilerParams(vmem_limit_bytes=16 * 2**20),
    )(update, momentum_new)


def solution(mesh):
    placed = (P(None, "rep", "fsdp", None), P("rep", "fsdp", None, None), P("rep", None, None))
    return jax.shard_map(
        local,
        mesh=mesh,
        in_specs=placed,
        out_specs=(P(None, None, "fsdp", None), P("rep", "fsdp", None, None)),
        check_vma=False,
    )
```

```python
import functools
import math

import jax
import jax.numpy as jnp
from jax import lax
from jax.experimental import pallas as pl
from jax.experimental.pallas import tpu as pltpu
from jax.sharding import PartitionSpec as P

RANK = 512
BLOCK = 128
ROWS_Y = 8
ROWS_X = 4
CHIPS = 16
PIECES = 8
ITERS = 5
LAG = 6

beta_decay = 0.95
coef_a = 3.4445
coef_b = -4.775
coef_c = 2.0315
epsilon = 1e-07
muon_scale = 0.2 * math.sqrt(max(RANK, BLOCK))

F32 = jnp.float32
BF16 = jnp.bfloat16
MESH = pl.DeviceIdType.MESH
OFFSETS = sorted(
    [(y, x) for y in range(ROWS_Y) for x in range(ROWS_X) if (y, x) != (0, 0)],
    key=lambda o: -(min(o[0], ROWS_Y - o[0]) + min(o[1], ROWS_X - o[1])),
)


DOWN = [7 + chip % 2 for chip in range(CHIPS)]
DOWN[8:14] = [8, 9, 9, 9, 8, 9]


def arrivals(chip, stream):
    found = []
    for back in range(1, CHIPS):
        start = (chip - back) % CHIPS if stream == 0 else (chip + back) % CHIPS
        if back <= (DOWN[start] if stream == 1 else CHIPS - 1 - DOWN[start]):
            found.append(back)
    return found


COUNTS = [[2 * len(arrivals(chip, stream)) for chip in range(CHIPS)] for stream in range(2)]
ITEMS = max(map(max, COUNTS))
for number_of in range(CHIPS):
    for stream_of in range(2):
        onto = COUNTS[stream_of][(number_of + 1 - 2 * stream_of) % CHIPS]
        assert arrivals(number_of, stream_of) == list(range(1, COUNTS[stream_of][number_of] // 2 + 1))
        assert LAG <= onto - 2 <= COUNTS[stream_of][number_of]
    assert COUNTS[0][number_of] + COUNTS[1][number_of] == 2 * (CHIPS - 1)


def look_up(first, second, chip, core):
    found = jnp.where(core == 0, first[0], second[0])
    for at in range(1, CHIPS):
        found = jnp.where(chip == at, jnp.where(core == 0, first[at], second[at]), found)
    return found


def split(value):
    high = value.astype(BF16)
    rest = value - high.astype(F32)
    mid = rest.astype(BF16)
    low = (rest - mid.astype(F32)).astype(BF16)
    return high, mid, low


def product(left, right):
    lh, lm, ll = left
    rh, rm, rl = right
    wide = jnp.concatenate([rh, rm], axis=1)
    main = jnp.dot(
        jnp.concatenate([lh, lm], axis=1), jnp.concatenate([wide, wide], axis=0), preferred_element_type=F32
    )
    rest = jnp.dot(
        jnp.concatenate([lh, ll], axis=1), jnp.concatenate([rl, rh], axis=0), preferred_element_type=F32
    )
    return main[:, :BLOCK] + (main[:, BLOCK:] + rest)


def gram(parts):
    high, mid, low = parts
    both = jnp.concatenate([high, mid], axis=1)
    dims = (((0,), (0,)), ((), ()))
    main = lax.dot_general(both, both, dims, preferred_element_type=F32)
    rest = lax.dot_general(high, low, dims, preferred_element_type=F32)
    cross = main[:BLOCK, BLOCK:] + main[BLOCK:, :BLOCK]
    return main[:BLOCK, :BLOCK] + (cross + (main[BLOCK:, BLOCK:] + (rest + rest.T)))


def orthogonalize(blends):
    row = lax.broadcasted_iota(jnp.int32, (BLOCK, BLOCK), 0)
    col = lax.broadcasted_iota(jnp.int32, (BLOCK, BLOCK), 1)
    eye = coef_a * (row == col).astype(F32)
    scales = [
        1.0 / (jnp.sqrt(jnp.sum(b * b, axis=(0, 1), keepdims=True)) + epsilon) for b in blends
    ]
    currents = blends
    for step in range(ITERS):
        parts = [split(y) for y in currents]
        grams = [gram(p) for p in parts]
        if step == 0:
            grams = [(g * v) * v for g, v in zip(grams, scales)]
        pieces = [split(g) for g in grams]
        squares = [product(p, p) for p in pieces]
        factors = [eye + coef_b * g + coef_c * s for g, s in zip(grams, squares)]
        if step == 0:
            factors = [f * v for f, v in zip(factors, scales)]
        currents = [product(p, split(f)) for p, f in zip(parts, factors)]
    return currents


def kernel(
    owner_hbm, gradient_hbm, momentum_hbm, update_ref, new_ref,
    owner_ref, gradient_ref, momentum_ref, packed, blocks, owned, returned, spread, load_sem,
    out_sem, in_sem, back_sem, home_sem, self_sem,
    go_sem, come_sem, give_sem, take_sem, first_sem,
):
    rep = lax.axis_index("rep")
    me = lax.axis_index("fsdp")
    core = lax.rem(rep, 2)
    chip = lax.div(rep, 2)
    way = 1 - 2 * core
    ahead = lax.rem(chip + way + CHIPS, CHIPS) * 2 + core
    behind = lax.rem(chip - way + CHIPS, CHIPS) * 2 + core
    twin = chip * 2 + 1 - core
    cross = lax.rem(chip - way + CHIPS, CHIPS) * 2 + 1 - core
    mine_y = lax.div(me, ROWS_X)
    mine_x = lax.rem(me, ROWS_X)
    fsdp_count, slot_count, depth, width = packed.shape
    layers, _, _, _ = gradient_ref.shape
    held = gradient_ref.shape[1]
    flat_rows = layers * held
    block_rows = flat_rows * depth
    slot_rows = fsdp_count * slot_count * depth

    def peer(offset):
        return lax.rem(mine_y + offset[0], ROWS_Y) * ROWS_X + lax.rem(mine_x + offset[1], ROWS_X)

    barrier = pltpu.get_barrier_semaphore()
    for offset in OFFSETS:
        pl.semaphore_signal(barrier, inc=1, device_id={"fsdp": peer(offset)}, device_id_type=MESH)
    for other in (ahead, behind, twin, cross):
        pl.semaphore_signal(barrier, inc=1, device_id={"rep": other}, device_id_type=MESH)

    loads = [
        pltpu.make_async_copy(source, target, load_sem.at[i])
        for i, (source, target) in enumerate(
            [(owner_hbm, owner_ref), (gradient_hbm, gradient_ref), (momentum_hbm, momentum_ref)])
    ]
    for load in loads:
        load.start()
    loads[0].wait()

    names = [owner_ref[j % held, j // held] for j in range(flat_rows)]

    def targets(shape, dim):
        at = lax.broadcasted_iota(jnp.int32, shape, dim)
        number = at // depth
        owner = jnp.zeros(shape, jnp.int32)
        for j in range(flat_rows):
            owner = jnp.where(number == j, names[j], owner)
        slot = jnp.zeros(shape, jnp.int32)
        for j in range(flat_rows):
            slot += jnp.where((number > j) & (owner == names[j]), 1, 0)
        return (owner * slot_count + slot) * depth + lax.rem(at, depth)

    across = targets((1, block_rows), 1)
    place = (lax.broadcasted_iota(jnp.int32, (slot_rows, block_rows), 0) == across).astype(F32).astype(BF16)
    loads[1].wait()
    packed[...] = jnp.dot(
        place, gradient_ref[...].reshape(block_rows, width), preferred_element_type=F32
    ).astype(BF16).reshape(packed.shape)

    pl.semaphore_wait(barrier, len(OFFSETS) + 4)

    def swap(source, landing, sent, got, offset):
        other = peer(offset)
        return pltpu.make_async_remote_copy(
            src_ref=source.at[other], dst_ref=landing.at[me], send_sem=sent, recv_sem=got,
            device_id={"fsdp": other}, device_id_type=MESH)

    def exchange(source, landing, sent, got):
        for offset in OFFSETS:
            swap(source, landing, sent, got, offset).start()
        stays = pltpu.make_async_copy(source.at[me], landing.at[me], self_sem)
        stays.start()
        return stays

    def exchanged(landing, sent, got):
        every = landing.at[pl.ds(0, len(OFFSETS))]
        return pltpu.make_async_remote_copy(
            src_ref=every, dst_ref=every, send_sem=sent, recv_sem=got,
            device_id={"fsdp": peer(OFFSETS[0])}, device_id_type=MESH)

    def finish(landing, sent, got, stays):
        stays.wait()
        exchanged(landing, sent, got).wait_recv()

    stays = exchange(packed, blocks, out_sem, in_sem)
    down = targets((block_rows, 1), 0)
    spread[...] = (lax.broadcasted_iota(jnp.int32, (block_rows, slot_rows), 1) == down).astype(F32).astype(BF16)
    finish(blocks, out_sem, in_sem, stays)

    loads[2].wait()
    blends = []
    for slot in range(slot_count):
        fresh = blocks[:, slot].reshape(RANK, width).astype(F32)
        carried = beta_decay * momentum_ref[0, slot].astype(F32) + fresh
        blends.append(fresh + beta_decay * carried)
    for slot, current in enumerate(orthogonalize(blends)):
        owned[:, slot] = (muon_scale * current).astype(BF16).reshape(fsdp_count, depth, width)

    stays = exchange(owned, returned, back_sem, home_sem)
    for slot in range(slot_count):
        fresh = blocks[:, slot].reshape(RANK, width).astype(F32)
        carried = beta_decay * momentum_ref[0, slot].astype(F32) + fresh
        new_ref[0, slot] = carried.astype(BF16)
    count = look_up(COUNTS[0], COUNTS[1], chip, core)
    ahead_count = look_up(COUNTS[0][1:] + COUNTS[0][:1], COUNTS[1][-1:] + COUNTS[1][:-1], chip, core)
    onward = ahead_count - 2
    finish(returned, back_sem, home_sem, stays)

    part = layers // PIECES
    def number(item):
        from_chip = lax.rem(chip - (lax.div(item, 2) + 1) * way + 2 * CHIPS, CHIPS)
        return from_chip * 2 + 1 - lax.rem(item, 2)

    def where(chunk, piece):
        return update_ref.at[pl.ds(piece * part, part), pl.ds(chunk * held, held)]

    def hop(item, at, piece):
        return pltpu.make_async_remote_copy(
            src_ref=at, dst_ref=at, send_sem=go_sem.at[item], recv_sem=come_sem.at[item, piece],
            device_id={"rep": ahead}, device_id_type=MESH)

    def share(at, sent, got):
        return pltpu.make_async_remote_copy(
            src_ref=at, dst_ref=at, send_sem=sent, recv_sem=got,
            device_id={"rep": twin}, device_id_type=MESH)

    half = layers // 2
    half_rows = block_rows // 2
    for side in range(2):
        update_ref[pl.ds(side * half, half), pl.ds(rep * held, held)] = jnp.dot(
            spread[pl.ds(side * half_rows, half_rows)], returned[...].reshape(slot_rows, width),
            preferred_element_type=F32,
        ).astype(BF16).reshape(half, held, depth, width)
        for piece in range(side * PIECES // 2, (side + 1) * PIECES // 2):
            at = where(rep, piece)
            for sem, target in ((0, ahead), (1, cross)):
                pltpu.make_async_remote_copy(
                    src_ref=at, dst_ref=at, send_sem=go_sem.at[sem], recv_sem=come_sem.at[1 - core, piece],
                    device_id={"rep": target}, device_id_type=MESH).start()
    for piece in range(PIECES):
        share(where(rep, piece), self_sem, first_sem).start()

    whole = update_ref.at[:, pl.ds(rep * held, held)]

    @pl.loop(0, onward)
    def _(item):
        chunk = number(item)
        for piece in range(PIECES):
            at = where(chunk, piece)
            hop(item, at, piece).wait_recv()
            hop(item + 2, at, piece).start()
            share(at, give_sem.at[item], take_sem.at[item]).start()

        @pl.when(item >= LAG)
        def _():
            share(whole, go_sem.at[item - LAG], self_sem).wait_send()
            share(whole, give_sem.at[item - LAG], self_sem).wait_send()

    @pl.loop(onward, count)
    def _(item):
        chunk = number(item)
        for piece in range(PIECES):
            at = where(chunk, piece)
            hop(item, at, piece).wait_recv()
            share(at, give_sem.at[item], take_sem.at[item]).start()

    share(whole, self_sem, first_sem).wait()
    for sem in (out_sem, back_sem):
        exchanged(packed, sem, sem).wait_send()

    @pl.loop(onward - LAG, ahead_count)
    def _(item):
        share(whole, go_sem.at[item], self_sem).wait_send()

    @pl.loop(onward - LAG, count)
    def _(item):
        share(whole, give_sem.at[item], self_sem).wait_send()

    @pl.loop(0, 2 * (CHIPS - 1) - count)
    def _(item):
        share(whole, self_sem, take_sem.at[item]).wait_recv()


def store_kernel(update_ref, new_ref, update_hbm, new_hbm, sems):
    copies = [
        pltpu.make_async_copy(update_ref, update_hbm, sems.at[0]),
        pltpu.make_async_copy(new_ref, new_hbm, sems.at[1]),
    ]
    for copy in copies:
        copy.start()
    for copy in copies:
        copy.wait()


def local(gradient, momentum, owners):
    layers, held, depth, width = gradient.shape
    slot_count = momentum.shape[1]
    fsdp_count = lax.axis_size("fsdp")
    rep_count = lax.axis_size("rep")
    vmem = pl.BlockSpec(memory_space=pltpu.VMEM)
    hbm = pl.BlockSpec(memory_space=pltpu.HBM)
    lanes = (fsdp_count, slot_count, depth, width)
    dma = pltpu.SemaphoreType.DMA
    update, momentum_new = pl.pallas_call(
        kernel,
        out_shape=(
            jax.ShapeDtypeStruct((layers, held * rep_count, depth, width), BF16),
            jax.ShapeDtypeStruct(momentum.shape, BF16),
        ),
        in_specs=[hbm, hbm, hbm],
        out_specs=(vmem, vmem),
        scratch_shapes=[
            pltpu.SMEM((held, layers), jnp.int32),
            pltpu.VMEM(gradient.shape, BF16),
            pltpu.VMEM(momentum.shape, BF16),
            pltpu.VMEM(lanes, BF16),
            pltpu.VMEM(lanes, BF16),
            pltpu.VMEM(lanes, BF16),
            pltpu.VMEM(lanes, BF16),
            pltpu.VMEM((layers * held * depth, fsdp_count * slot_count * depth), BF16),
            dma((3,)),
            dma, dma, dma, dma, dma,
            dma((ITEMS,)),
            dma((ITEMS, PIECES)),
            dma((ITEMS,)), dma((ITEMS,)),
            dma,
        ],
        compiler_params=pltpu.CompilerParams(
            collective_id=1, has_side_effects=True, vmem_limit_bytes=40 * 2**20),
        cost_estimate=pl.CostEstimate(flops=3 * 10**9, bytes_accessed=2**23, transcendentals=0),
    )(*(pltpu.with_memory_space_constraint(a, pltpu.HBM) for a in (owners[:, :, 0], gradient, momentum)))
    return pl.pallas_call(
        store_kernel,
        out_shape=(
            jax.ShapeDtypeStruct(update.shape, BF16),
            jax.ShapeDtypeStruct(momentum_new.shape, BF16),
        ),
        in_specs=[vmem, vmem],
        out_specs=(hbm, hbm),
        scratch_shapes=[dma((2,))],
        compiler_params=pltpu.CompilerParams(vmem_limit_bytes=16 * 2**20),
    )(update, momentum_new)


def solution(mesh):
    placed = (P(None, "rep", "fsdp", None), P("rep", "fsdp", None, None), P("rep", None, None))
    return jax.shard_map(
        local,
        mesh=mesh,
        in_specs=placed,
        out_specs=(P(None, None, "fsdp", None), P("rep", "fsdp", None, None)),
        check_vma=False,
    )
```
